128 devices in a mesh: rep: 4 (over x), ten: 32 (over y, z, core).
Axes of the slice: x: 4, y: 4, z: 4, core: 2. Of those that a mesh axis runs over, the one named last changes fastest.
Arguments:
- amplitudes: bfloat16 [32, 32, 1024, 128], P('ten', 'rep'), may hold values from -6 to 6
- integrals: bfloat16 [32, 1024, 32, 128], P('rep', 'ten'), may hold values from -0.125 to 0.125
- pair_irreps: int32 [2], replicated, may hold values from 0 to 7
Outputs:
- cycle: bfloat16 [32, 32, 1024, 128], P('ten', 'rep')
The draws below stay inside these ranges and needn't reach their ends.
All inputs are finite; a program needn't handle non-finite values.
Results may differ from the reference program's by a relative error of at most 0.001.
Values may be sent and summed in bfloat16 or wider, within the bound.
No kernel may reach another device: no remote copies, remote signals or barrier semaphores. Data moves between devices by JAX's collectives and lax.ppermute only.
A program may use at most 192 MiB of HBM per device.

```python
import jax
import jax.numpy as jnp
from jax import lax

NB = 128
V = 1024
NI = 32
NK = 32
NJ = 32


def with_spikes(entries, own_key, source, target, blocks, factor):
    owner, partner = [(jnp.arange(entries.shape[dim]) // (entries.shape[dim] // blocks)).reshape([-1 if axis == dim else 1 for axis in range(entries.ndim)]) for dim in (source, target)]
    chosen = jax.random.permutation(own_key, blocks)[partner]
    strong = (owner == chosen) | (owner == (partner + blocks // 2) % blocks)
    return jnp.where(strong, factor * entries, entries)


def level_of(own_key, shape, cuts, smallest, high):
    level = 1.0
    for position, blocks in cuts:
        heights = jax.random.uniform(jax.random.fold_in(jax.random.fold_in(own_key, 6), position), (blocks,), jnp.float32, smallest / len(cuts), high / len(cuts))
        level = level * jnp.repeat(jnp.exp(heights), shape[position] // blocks).reshape((-1,) + (1,) * (len(shape) - 1 - position))
    return level


def scatter_about(key, shape, spread, bound, cuts=(), dtype=jnp.bfloat16):
    entries = spread * jax.random.normal(key, shape, jnp.float32)
    if cuts:
        entries = entries * level_of(key, shape, cuts, -0.22, 0.18)
    return jnp.clip(entries, -bound, bound).astype(dtype)


def heavy_noise(stream_key, shape, spread, bound, cuts, heavy, dtype=jnp.bfloat16):
    entries = spread * jax.random.normal(stream_key, shape, jnp.float32)
    if cuts:
        entries = entries * level_of(stream_key, shape, cuts, -0.22, 0.18)
    return jnp.clip(with_spikes(entries, jax.random.fold_in(stream_key, 3), *heavy), -bound, bound).astype(dtype)


def setup_inputs(seed: int = 0) -> dict:
    keys = jax.random.split(jax.random.key(seed), 4)
    return {
        "amplitudes": scatter_about(keys[0], (NI, NK, V, NB), 1.0, 6.0, ((0, 32), (1, 4))),
        "integrals": heavy_noise(keys[1], (NK, V, NJ, NB), (NK * NB) ** -0.5, 0.125, ((0, 4), (1, 32)), (0, 2, 4, 2.0)),
        "pair_irreps": jax.random.randint(keys[2], (2,), 0, 8).astype(jnp.int32),
    }


def reference(amplitudes, integrals, pair_irreps):
    pair_xor = jnp.bitwise_xor(pair_irreps[0], pair_irreps[1])
    pieces = []
    for irrep_index in range(8):
        amp_rows = amplitudes[:, :, irrep_index * NB:(irrep_index + 1) * NB].astype(jnp.float32)
        first_row = (jnp.bitwise_xor(irrep_index, pair_xor) * NB).astype(jnp.int32)
        chosen = lax.dynamic_slice_in_dim(integrals, first_row, NB, 1).astype(jnp.float32)
        pieces.append(jnp.einsum("ikac,kcjb->ijab", amp_rows, chosen))
    return jnp.concatenate(pieces, axis=2).astype(jnp.bfloat16)
```

```python
import jax
import jax.numpy as jnp
from jax import lax
from jax.sharding import PartitionSpec as P

IRREPS = 8
CHUNKS = 4


def shift_rep(array, distance):
    n = lax.axis_size("rep")
    return lax.ppermute(array, "rep", [(s, (s + distance) % n) for s in range(n)])


def flip_ten(array, mask):
    return lax.ppermute(array, "ten", [(s, s ^ mask) for s in range(lax.axis_size("ten"))])


def exchange_irreps(array, groups):
    return lax.all_to_all(
        array, "ten", split_axis=0, concat_axis=0, axis_index_groups=groups, tiled=True
    )


def gather_rep(block):
    half = block.shape[0] // 2
    from_left = shift_rep(block, 1)
    from_right = shift_rep(block, -1)
    far = jnp.concatenate([shift_rep(from_left[:half], 1), shift_rep(from_right[half:], -1)], axis=0)
    return jnp.concatenate([block, from_left, from_right, far], axis=1)


def per_device(amplitudes, integrals, pair_irreps):
    pair_xor = jnp.bitwise_xor(pair_irreps[0], pair_irreps[1])
    ten = lax.axis_size("ten")
    quarters = ten // IRREPS
    groups = [[g * quarters + q for g in range(IRREPS)] for q in range(quarters)]
    column = lax.axis_index("rep")
    ranks = lax.axis_size("rep")
    quarter = lax.axis_index("ten") % quarters

    nk, rows, js = amplitudes.shape[1], amplitudes.shape[3], integrals.shape[2] // ranks
    amps = amplitudes.reshape(nk, IRREPS, rows, rows)
    order = jnp.bitwise_xor(jnp.arange(IRREPS), pair_xor)
    by_group = jnp.take(amps.transpose(1, 0, 2, 3), order, axis=0)

    by_j = integrals.transpose(2, 0, 1, 3)

    def j_block(distance):
        return lax.dynamic_slice_in_dim(by_j, ((column + distance) % ranks) * js, js, 0)

    pieces = [j_block(0), shift_rep(j_block(1), 1), shift_rep(j_block(3), -1), shift_rep(j_block(2), 2)]
    held = jnp.concatenate(pieces, axis=1)
    other = flip_ten(held, 2)
    upper = (quarter // 2) == 1
    pair = jnp.stack([jnp.where(upper, other, held), jnp.where(upper, held, other)], axis=2)
    across = flip_ten(pair, 1)
    odd = (quarter % 2) == 1
    block = jnp.stack([jnp.where(odd, across, pair), jnp.where(odd, pair, across)], axis=3)
    chosen = block.reshape(js, nk * ranks, rows, rows)

    mine = exchange_irreps(by_group, groups)
    step = rows // CHUNKS
    outs = []
    for chunk in range(CHUNKS):
        part = gather_rep(mine[:, :, chunk * step:(chunk + 1) * step])
        sums = jnp.einsum("ikac,jkcb->ijab", part, chosen, preferred_element_type=jnp.float32)
        outs.append(exchange_irreps(sums.astype(jnp.bfloat16), groups))
    result = jnp.take(jnp.concatenate(outs, axis=2), order, axis=0)
    return result.transpose(1, 0, 2, 3).reshape(amplitudes.shape)


def solution(mesh):
    in_specs = (P("ten", "rep", None, None), P("rep", "ten", None, None), P())
    return jax.shard_map(
        per_device, mesh=mesh, in_specs=in_specs, out_specs=in_specs[0], check_vma=False
    )
```

```python
import functools

import jax
import jax.numpy as jnp
from jax import lax
from jax.experimental import pallas as pl
from jax.experimental.pallas import tpu as pltpu
from jax.sharding import PartitionSpec as P

IRREPS = 8
STEPS = (64, 64)
VMEM_PRODUCT = 60
MIB = 1 << 20


def shift_rep(array, distance):
    n = lax.axis_size("rep")
    return lax.ppermute(array, "rep", [(s, (s + distance) % n) for s in range(n)])


def flip_ten(array, mask):
    return lax.ppermute(array, "ten", [(s, s ^ mask) for s in range(lax.axis_size("ten"))])


def exchange_irreps(array, groups):
    return lax.all_to_all(
        array, "ten", split_axis=0, concat_axis=0, axis_index_groups=groups, tiled=True
    )


def params(limit):
    return pltpu.CompilerParams(vmem_limit_bytes=limit * MIB)


def cost(flops, moved):
    return pl.CostEstimate(flops=0, bytes_accessed=0, transcendentals=0)


def order_body(xor_ref, amps_ref, *out_refs):
    place = 0
    for ref in out_refs:
        step = ref.shape[2]
        ref[0] = amps_ref[:, 0, place:place + step]
        place += step


def order_amps(amps, pair_xor, steps):
    nk, irreps, rows, cols = amps.shape
    return pl.pallas_call(
        order_body,
        out_shape=[jax.ShapeDtypeStruct((irreps, nk, step, cols), amps.dtype) for step in steps],
        grid_spec=pltpu.PrefetchScalarGridSpec(
            num_scalar_prefetch=1,
            grid=(irreps,),
            in_specs=[pl.BlockSpec((nk, 1, rows, cols), lambda g, px: (0, jnp.bitwise_xor(g, px[0]), 0, 0))],
            out_specs=[pl.BlockSpec((1, nk, step, cols), lambda g, px: (g, 0, 0, 0)) for step in steps],
        ),
        compiler_params=params(16),
        cost_estimate=cost(0, 2 * amps.size * 2),
        name="order_amps",
    )(pair_xor.reshape(1), amps)


def by_j_body(ranks, w_ref, out_ref):
    rows, js, cols = w_ref.shape[1:]
    share = js // ranks
    moved = jnp.swapaxes(w_ref[0].astype(jnp.float32), 0, 1).astype(w_ref.dtype)
    for j in range(js):
        place = (j % share) * cols
        out_ref[j // share, 0, :, place:place + cols] = moved[j]


def integrals_by_j(integrals, ranks):
    nk, rows, js, cols = integrals.shape
    share = js // ranks
    return pl.pallas_call(
        functools.partial(by_j_body, ranks),
        out_shape=jax.ShapeDtypeStruct((ranks, nk, rows, share * cols), integrals.dtype),
        grid=(nk,),
        in_specs=[pl.BlockSpec((1, rows, js, cols), lambda k: (k, 0, 0, 0))],
        out_specs=pl.BlockSpec((ranks, 1, rows, share * cols), lambda k: (0, k, 0, 0)),
        compiler_params=params(16),
        cost_estimate=cost(0, 2 * integrals.size * 2),
        name="integrals_by_j",
    )(integrals)


def product_body(plan, blocks, rows_of, has_sum, quarter_ref, *refs):
    count = len(plan)
    pieces, w_refs = refs[:count], refs[count:count + 4 * len(blocks)]
    sum_refs = refs[count + 4 * len(blocks):][:1] if has_sum else ()
    out_ref, lhs, chosen, total, piece_sems, w_sems = refs[-6:]
    nk, rows, width = w_refs[0].shape
    cols = lhs.shape[2] // nk
    quarter = quarter_ref[0]

    copies = {}
    for slot, block in enumerate(blocks):
        copies[block] = []
        for d in range(4):
            place = pl.multiple_of(jnp.bitwise_xor(quarter, d) * rows, rows)
            copies[block].append(
                pltpu.make_async_copy(
                    w_refs[4 * slot + d],
                    chosen.at[pl.ds(slot * nk, nk), pl.ds(place, rows), :],
                    w_sems.at[4 * slot + d],
                )
            )
    for n, ((row, block), ref) in enumerate(zip(plan, pieces)):
        slot = blocks.index(block)
        for k in range(nk):
            copies[block].append(
                pltpu.make_async_copy(
                    ref.at[:, k],
                    lhs.at[pl.ds(slot * rows_of + row, ref.shape[0]), :, pl.ds(k * cols, cols)],
                    piece_sems.at[n * nk + k],
                )
            )
    for block in blocks:
        for copy in copies[block]:
            copy.start()
    for slot, block in enumerate(blocks):
        for copy in copies[block]:
            copy.wait()
        left = lhs[slot * rows_of:(slot + 1) * rows_of].reshape(-1, nk * cols)
        right = chosen[slot * nk:(slot + 1) * nk].reshape(nk * 4 * rows, width)
        sums = jnp.dot(left, right, preferred_element_type=jnp.float32)
        if slot == 0:
            if has_sum:
                sums = sums + sum_refs[0][...]
        else:
            sums = sums + total[...]
        if slot < len(blocks) - 1:
            total[...] = sums
        elif out_ref.dtype == jnp.float32:
            out_ref[...] = sums
        else:
            ni, js, step, _ = out_ref.shape
            for j in range(js):
                out_ref[:, j] = sums[:, j * cols:(j + 1) * cols].astype(out_ref.dtype).reshape(ni, step, cols)


def product(pieces, plan, chosen, blocks, quarter, sums=None, last=True):
    nk, step, cols = pieces[0].shape[1:]
    ni = IRREPS
    rows, width = chosen[0][0].shape[1:]
    js = width // cols
    w_parts = [part for block in blocks for part in chosen[block]]
    operands = [quarter.reshape(1), *pieces, *w_parts]
    in_specs = [pl.BlockSpec(memory_space=pltpu.SMEM)]
    in_specs += [pl.BlockSpec(memory_space=pl.ANY)] * (len(operands) - 1)
    if sums is not None:
        in_specs.append(pl.BlockSpec(memory_space=pltpu.VMEM))
        operands.append(sums)
    if last:
        out_shape = jax.ShapeDtypeStruct((ni, js, step, cols), pieces[0].dtype)
    else:
        out_shape = jax.ShapeDtypeStruct((ni * step, width), jnp.float32)
    depth = nk * 4 * rows * len(blocks)
    return pl.pallas_call(
        functools.partial(product_body, plan, blocks, ni, sums is not None),
        out_shape=out_shape,
        in_specs=in_specs,
        out_specs=pl.BlockSpec(memory_space=pltpu.VMEM),
        scratch_shapes=[
            pltpu.VMEM((ni * len(blocks), step, nk * cols), pieces[0].dtype),
            pltpu.VMEM((nk * len(blocks), 4 * rows, width), pieces[0].dtype),
            pltpu.VMEM((ni * step, width), jnp.float32),
            pltpu.SemaphoreType.DMA((len(pieces) * nk,)),
            pltpu.SemaphoreType.DMA((len(w_parts),)),
        ],
        compiler_params=params(VMEM_PRODUCT),
        cost_estimate=cost(2 * ni * step * depth * width, 2 * depth * width + 2 * ni * step * depth),
        name="product",
    )(*operands)


def place_body(offset, xor_ref, part_ref, *refs):
    out_ref, sems = refs[-2:]
    irreps, _, step, _ = part_ref.shape
    copies = [
        pltpu.make_async_copy(
            part_ref.at[g],
            out_ref.at[:, jnp.bitwise_xor(g, xor_ref[0]), offset:offset + step],
            sems.at[g],
        )
        for g in range(irreps)
    ]
    for copy in copies:
        copy.start()
    for copy in copies:
        copy.wait()


def place_irreps(part, pair_xor, rows, offset, result):
    irreps, js, step, cols = part.shape
    operands = [pair_xor.reshape(1), part]
    aliases = {}
    if result is not None:
        operands.append(result)
        aliases = {2: 0}
    return pl.pallas_call(
        functools.partial(place_body, offset),
        out_shape=jax.ShapeDtypeStruct((js, irreps, rows, cols), part.dtype),
        grid_spec=pltpu.PrefetchScalarGridSpec(
            num_scalar_prefetch=1,
            grid=(1,),
            in_specs=[pl.BlockSpec(memory_space=pl.ANY)] * (len(operands) - 1),
            out_specs=pl.BlockSpec(memory_space=pl.ANY),
            scratch_shapes=[pltpu.SemaphoreType.DMA((irreps,))],
        ),
        input_output_aliases=aliases,
        compiler_params=params(16),
        cost_estimate=cost(0, 2 * part.size * 2),
        name="place_irreps",
    )(*operands)


def after(values, *earlier):
    return lax.optimization_barrier((values, earlier))[0]


def per_device(amplitudes, integrals, pair_irreps):
    pair_xor = jnp.bitwise_xor(pair_irreps[0], pair_irreps[1])
    quarters = lax.axis_size("ten") // IRREPS
    groups = [
        [g * quarters + (q ^ (g % 2 * quarters // 2)) for g in range(IRREPS)] for q in range(quarters)
    ]
    ranks = lax.axis_size("rep")
    column = lax.axis_index("rep")
    quarter = lax.axis_index("ten") % quarters
    nk, rows = amplitudes.shape[1], amplitudes.shape[3]
    half = IRREPS // 2

    by_j = integrals_by_j(integrals, ranks)
    amplitudes, by_j = lax.optimization_barrier((amplitudes, by_j))
    by_group = order_amps(amplitudes.reshape(nk, IRREPS, rows, rows), pair_xor, STEPS)

    def for_rank(distance):
        return lax.dynamic_index_in_dim(by_j, (column + distance) % ranks, 0, keepdims=False)

    near = for_rank(0)
    arrived = [near, shift_rep(for_rank(1), 1), shift_rep(for_rank(3), -1), shift_rep(for_rank(2), 2)]
    zl = [flip_ten(part, 2) for part in arrived]
    core = [flip_ten(part, 1) for part in arrived]
    both = [flip_ten(part, 1) for part in zl]

    first = exchange_irreps(by_group[0], groups)
    first, core[1], core[2], arrived[3], both[0] = lax.optimization_barrier(
        (first, core[1], core[2], arrived[3], both[0])
    )
    second = exchange_irreps(after(by_group[1], first), groups)

    left, right = shift_rep(first, 1), shift_rep(first, -1)
    left2, right2 = shift_rep(second, 1), shift_rep(second, -1)
    left, right, zl[1], zl[2] = lax.optimization_barrier((left, right, zl[1], zl[2]))
    low, high = shift_rep(left[:half], 1), shift_rep(right[half:], -1)
    left2, right2, zl[3], both[1], both[2] = lax.optimization_barrier((left2, right2, zl[3], both[1], both[2]))
    low, high, left2, right2 = lax.optimization_barrier((low, high, left2, right2))
    low2, high2 = shift_rep(left2[:half], 1), shift_rep(right2[half:], -1)
    chosen = [(arrived[n], core[n], zl[n], both[n]) for n in range(ranks)]

    halves = ((0, 3), (half, 3))
    wholes = ((0, 0), (0, 1), (0, 2))
    out = product((first, left, right, low, high), wholes + halves, chosen, (0, 1, 2, 3), quarter)
    sums = product((second, left2, right2), wholes, chosen, (0, 1, 2), quarter, last=False)
    low2, high2, sums, out = lax.optimization_barrier((low2, high2, sums, out))
    back = exchange_irreps(out, groups)
    out2 = product((low2, high2), halves, chosen, (3,), quarter, sums=sums)
    back, out2 = lax.optimization_barrier((back, out2))
    back2 = exchange_irreps(out2, groups)
    result = place_irreps(back, pair_xor, rows, 0, None)
    result = place_irreps(back2, pair_xor, rows, STEPS[0], result)
    return result.reshape(amplitudes.shape)


def solution(mesh):
    in_specs = (P("ten", "rep", None, None), P("rep", "ten", None, None), P())
    return jax.shard_map(
        per_device, mesh=mesh, in_specs=in_specs, out_specs=in_specs[0], check_vma=False
    )
```

```python
import functools

import jax
import jax.numpy as jnp
from jax import lax
from jax.experimental import pallas as pl
from jax.experimental.pallas import tpu as pltpu
from jax.sharding import PartitionSpec as P

IRREPS = 8
STEPS = (64, 64)
VMEM_PRODUCT = 44
AHEAD = 2
MIB = 1 << 20


def shift_rep(array, distance):
    n = lax.axis_size("rep")
    return lax.ppermute(array, "rep", [(s, (s + distance) % n) for s in range(n)])


def flip_ten(array, mask):
    return lax.ppermute(array, "ten", [(s, s ^ mask) for s in range(lax.axis_size("ten"))])


def exchange_irreps(array, groups):
    return lax.all_to_all(
        array, "ten", split_axis=0, concat_axis=0, axis_index_groups=groups, tiled=True
    )


def params(limit):
    return pltpu.CompilerParams(vmem_limit_bytes=limit * MIB)


def cost(flops, moved):
    return pl.CostEstimate(flops=0, bytes_accessed=0, transcendentals=0)


def order_body(offset, pair_ref, amps_ref, out_ref, sems):
    irreps, _, step, _ = out_ref.shape
    pair_xor = jnp.bitwise_xor(pair_ref[0], pair_ref[1])
    copies = [
        pltpu.make_async_copy(
            amps_ref.at[:, jnp.bitwise_xor(g, pair_xor), offset:offset + step],
            out_ref.at[g],
            sems.at[g],
        )
        for g in range(irreps)
    ]
    for copy in copies:
        copy.start()
    for copy in copies:
        copy.wait()


def order_amps(amps, pair_irreps, offset, step):
    nk, irreps, _, cols = amps.shape
    return pl.pallas_call(
        functools.partial(order_body, offset),
        out_shape=pltpu.VMEM((irreps, nk, step, cols), amps.dtype),
        in_specs=[pl.BlockSpec(memory_space=pltpu.SMEM), pl.BlockSpec(memory_space=pl.ANY)],
        out_specs=pl.BlockSpec(memory_space=pltpu.VMEM),
        scratch_shapes=[pltpu.SemaphoreType.DMA((irreps,))],
        compiler_params=params(16),
        cost_estimate=cost(0, 0),
        name="order_amps",
    )(pair_irreps, pltpu.with_memory_space_constraint(amps, pltpu.HBM))


def by_j_body(ranks, w_ref, *refs):
    out_refs, moved = refs[:-1], refs[-1]
    rows, js, cols = w_ref.shape[1:]
    share = js // ranks
    moved[...] = jnp.swapaxes(w_ref[0].astype(jnp.float32), 0, 1).astype(w_ref.dtype)
    for distance, ref in enumerate(out_refs):
        first = lax.rem(lax.axis_index("rep") + distance, ranks) * share
        for j in range(share):
            ref[0, :, j * cols:(j + 1) * cols] = moved[first + j]


def integrals_by_j(integrals, ranks):
    nk, rows, js, cols = integrals.shape
    wide = js // ranks * cols
    return pl.pallas_call(
        functools.partial(by_j_body, ranks),
        out_shape=[jax.ShapeDtypeStruct((nk, rows, wide), integrals.dtype)] * ranks,
        grid=(nk,),
        in_specs=[pl.BlockSpec((1, rows, js, cols), lambda k: (k, 0, 0, 0))],
        out_specs=[pl.BlockSpec((1, rows, wide), lambda k: (k, 0, 0))] * ranks,
        scratch_shapes=[pltpu.VMEM((js, rows, cols), integrals.dtype)],
        compiler_params=params(16),
        cost_estimate=cost(0, 0),
        name="integrals_by_j",
    )(integrals)


def product_body(plan, blocks, has_sum, quarter_ref, *refs):
    count = len(plan)
    pieces, w_refs = refs[:count], refs[count:count + 4 * len(blocks)]
    sum_refs = refs[count + 4 * len(blocks):][:1] if has_sum else ()
    out_ref, lhs, chosen, total, piece_sems, w_sems = refs[-6:]
    nk, rows, width = w_refs[0].shape
    ni, _, step, cols = pieces[0].shape
    quarter = quarter_ref[0]

    def copies(slot):
        found = []
        for d in range(4):
            place = pl.multiple_of(jnp.bitwise_xor(quarter, d) * rows, rows)
            found.append(
                pltpu.make_async_copy(
                    w_refs[4 * slot + d],
                    chosen.at[pl.ds(slot * nk, nk), pl.ds(place, rows), :],
                    w_sems.at[4 * slot + d],
                )
            )
        n = plan.index(blocks[slot])
        found.append(
            pltpu.make_async_copy(pieces[n], lhs.at[pl.ds(slot * ni, ni)], piece_sems.at[slot])
        )
        return found

    waiting = [copies(slot) for slot in range(len(blocks))]
    for slot in range(min(AHEAD, len(blocks))):
        for copy in waiting[slot]:
            copy.start()
    for slot in range(len(blocks)):
        for copy in waiting[slot]:
            copy.wait()
        if slot + AHEAD < len(blocks):
            for copy in waiting[slot + AHEAD]:
                copy.start()
        left = jnp.concatenate(
            [lhs[slot * ni:(slot + 1) * ni, k].reshape(ni * step, cols) for k in range(nk)], axis=1
        )
        right = chosen[slot * nk:(slot + 1) * nk].reshape(nk * 4 * rows, width)
        sums = jnp.dot(left, right, preferred_element_type=jnp.float32)
        if slot == 0:
            if has_sum:
                sums = sums + sum_refs[0][...]
        else:
            sums = sums + total[...]
        if slot < len(blocks) - 1:
            total[...] = sums
        elif out_ref.dtype == jnp.float32:
            out_ref[...] = sums
        else:
            for j in range(width // cols):
                out_ref[:, j] = sums[:, j * cols:(j + 1) * cols].astype(out_ref.dtype).reshape(ni, step, cols)


def product(pieces, plan, chosen, blocks, quarter, sums=None, last=True):
    nk, step, cols = pieces[0].shape[1:]
    ni = IRREPS
    rows, width = chosen[0][0].shape[1:]
    js = width // cols
    w_parts = [part for block in blocks for part in chosen[block]]
    if sums is None:
        pieces = [pltpu.with_memory_space_constraint(piece, pltpu.HBM) for piece in pieces]
        w_parts = [pltpu.with_memory_space_constraint(part, pltpu.HBM) for part in w_parts]
    operands = [quarter.reshape(1), *pieces, *w_parts]
    in_specs = [pl.BlockSpec(memory_space=pltpu.SMEM)]
    in_specs += [pl.BlockSpec(memory_space=pl.ANY)] * (len(operands) - 1)
    if sums is not None:
        in_specs.append(pl.BlockSpec(memory_space=pltpu.VMEM))
        operands.append(sums)
    if last:
        out_shape = [jax.ShapeDtypeStruct((ni, js, step, cols), chosen[0][0].dtype)]
    else:
        out_shape = [jax.ShapeDtypeStruct((ni * step, width), jnp.float32)]
    depth = nk * 4 * rows * len(blocks)
    return pl.pallas_call(
        functools.partial(product_body, plan, blocks, sums is not None),
        out_shape=out_shape,
        in_specs=in_specs,
        out_specs=[pl.BlockSpec(memory_space=pltpu.VMEM)],
        scratch_shapes=[
            pltpu.VMEM((ni * len(blocks), nk, step, cols), chosen[0][0].dtype),
            pltpu.VMEM((nk * len(blocks), 4 * rows, width), chosen[0][0].dtype),
            pltpu.VMEM((ni * step, width), jnp.float32),
            pltpu.SemaphoreType.DMA((len(pieces),)),
            pltpu.SemaphoreType.DMA((len(w_parts),)),
        ],
        compiler_params=params(VMEM_PRODUCT),
        cost_estimate=cost(2 * ni * step * depth * width, 2 * depth * width + 2 * ni * step * depth),
        name="product",
    )(*operands)


def place_body(offset, xor_ref, part_ref, *refs):
    out_ref, sems = refs[-2:]
    irreps, _, step, _ = part_ref.shape
    copies = [
        pltpu.make_async_copy(
            part_ref.at[g],
            out_ref.at[:, jnp.bitwise_xor(g, xor_ref[0]), offset:offset + step],
            sems.at[g],
        )
        for g in range(irreps)
    ]
    for copy in copies:
        copy.start()
    for copy in copies:
        copy.wait()


def place_irreps(part, pair_xor, rows, offset, result):
    irreps, js, step, cols = part.shape
    operands = [pair_xor.reshape(1), part]
    aliases = {}
    if result is not None:
        aliases = {len(operands): 0}
        operands.append(result)
    return pl.pallas_call(
        functools.partial(place_body, offset),
        out_shape=jax.ShapeDtypeStruct((js, irreps, rows, cols), part.dtype),
        in_specs=[pl.BlockSpec(memory_space=pltpu.SMEM)]
        + [pl.BlockSpec(memory_space=pl.ANY)] * (len(operands) - 1),
        out_specs=pl.BlockSpec(memory_space=pl.ANY),
        scratch_shapes=[pltpu.SemaphoreType.DMA((irreps,))],
        input_output_aliases=aliases,
        compiler_params=params(16),
        cost_estimate=cost(0, 0),
        name="place_irreps",
    )(*operands)


def after(values, *earlier):
    return lax.optimization_barrier((values, earlier))[0]


def per_device(amplitudes, integrals, pair_irreps):
    quarters = lax.axis_size("ten") // IRREPS
    groups = [
        [g * quarters + (q ^ (g % 2 * quarters // 2)) for g in range(IRREPS)] for q in range(quarters)
    ]
    ranks = lax.axis_size("rep")
    quarter = lax.axis_index("ten") % quarters
    nk, rows = amplitudes.shape[1], amplitudes.shape[3]

    by_j = integrals_by_j(integrals, ranks)
    amplitudes, by_j = lax.optimization_barrier((amplitudes, by_j))
    amps = amplitudes.reshape(nk, IRREPS, rows, rows)
    by_group = order_amps(amps, pair_irreps, 0, STEPS[0])

    near = by_j[0]
    arrived = [near, shift_rep(by_j[1], 1), shift_rep(by_j[3], -1), shift_rep(by_j[2], 2)]
    zl = [flip_ten(part, 2) for part in arrived]
    core = [flip_ten(part, 1) for part in arrived]
    both = [flip_ten(part, 1) for part in zl]

    first = exchange_irreps(by_group, groups)
    by_group2 = order_amps(after(amps, core[1]), pair_irreps, STEPS[0], STEPS[1])
    first, core[1], core[2], arrived[3], zl[0], by_group2 = lax.optimization_barrier(
        (first, core[1], core[2], arrived[3], zl[0], by_group2)
    )
    core[3], zl[3] = flip_ten(arrived[3], 1), flip_ten(arrived[3], 2)
    both[0] = flip_ten(zl[0], 1)
    by_group2, core[3] = lax.optimization_barrier((by_group2, core[3]))
    second = exchange_irreps(by_group2, groups)

    left, right = shift_rep(first, 1), shift_rep(first, -1)
    right2 = shift_rep(second, -1)
    left, right, zl[1] = lax.optimization_barrier((left, right, zl[1]))
    far = shift_rep(left, 1)
    both[1] = flip_ten(zl[1], 1)
    left2 = shift_rep(after(second, both[1]), 1)
    far2 = shift_rep(right2, -1)
    both[2], both[3] = flip_ten(zl[2], 1), flip_ten(zl[3], 1)
    chosen = [(arrived[n], core[n], zl[n], both[n]) for n in range(ranks)]

    (sums,) = product((first, left, right), (0, 1, 2), chosen, (0, 1, 2), quarter, last=False)
    far, sums = lax.optimization_barrier((far, sums))
    (out,) = product((far,), (3,), chosen, (3,), quarter, sums=sums)
    back = exchange_irreps(out, groups)
    (sums,) = product((second, right2), (0, 2), chosen, (0, 2), quarter, last=False)
    left2, far2, sums = lax.optimization_barrier((left2, far2, sums))
    (out2,) = product((left2, far2), (1, 3), chosen, (1, 3), quarter, sums=sums)
    pair_xor = jnp.bitwise_xor(pair_irreps[0], pair_irreps[1])
    back, out2 = lax.optimization_barrier((back, out2))
    back2 = exchange_irreps(out2, groups)
    result = place_irreps(back, pair_xor, rows, 0, None)
    result = place_irreps(back2, pair_xor, rows, STEPS[0], result)
    return result.reshape(amplitudes.shape)


def solution(mesh):
    in_specs = (P("ten", "rep", None, None), P("rep", "ten", None, None), P())
    return jax.shard_map(
        per_device, mesh=mesh, in_specs=in_specs, out_specs=in_specs[0], check_vma=False
    )
```

```python
import functools

import jax
import jax.numpy as jnp
from jax import lax
from jax.experimental import pallas as pl
from jax.experimental.pallas import tpu as pltpu
from jax.sharding import PartitionSpec as P

IRREPS = 8
STEPS = (64, 64)
VMEM_PRODUCT = 24
AHEAD = 2
MIB = 1 << 20


def shift_rep(array, distance):
    n = lax.axis_size("rep")
    return lax.ppermute(array, "rep", [(s, (s + distance) % n) for s in range(n)])


def flip_ten(array, mask):
    return lax.ppermute(array, "ten", [(s, s ^ mask) for s in range(lax.axis_size("ten"))])


def exchange_irreps(array, groups):
    return lax.all_to_all(
        array, "ten", split_axis=0, concat_axis=0, axis_index_groups=groups, tiled=True
    )


def params(limit):
    return pltpu.CompilerParams(vmem_limit_bytes=limit * MIB)


def cost(flops, moved):
    return pl.CostEstimate(flops=0, bytes_accessed=0, transcendentals=0)


def order_body(offset, pair_ref, amps_ref, out_ref, sems):
    irreps, _, step, _ = out_ref.shape
    pair_xor = jnp.bitwise_xor(pair_ref[0], pair_ref[1])
    copies = [
        pltpu.make_async_copy(
            amps_ref.at[:, jnp.bitwise_xor(g, pair_xor), offset:offset + step],
            out_ref.at[g],
            sems.at[g],
        )
        for g in range(irreps)
    ]
    for copy in copies:
        copy.start()
    for copy in copies:
        copy.wait()


def order_amps(amps, pair_irreps, offset, step):
    nk, irreps, _, cols = amps.shape
    return pl.pallas_call(
        functools.partial(order_body, offset),
        out_shape=pltpu.VMEM((irreps, nk, step, cols), amps.dtype),
        in_specs=[pl.BlockSpec(memory_space=pltpu.SMEM), pl.BlockSpec(memory_space=pl.ANY)],
        out_specs=pl.BlockSpec(memory_space=pltpu.VMEM),
        scratch_shapes=[pltpu.SemaphoreType.DMA((irreps,))],
        compiler_params=params(16),
        cost_estimate=cost(0, 0),
        name="order_amps",
    )(pair_irreps, pltpu.with_memory_space_constraint(amps, pltpu.HBM))


def by_j_body(ranks, w_ref, *refs):
    out_refs, moved = refs[:-1], refs[-1]
    rows, js, cols = w_ref.shape[1:]
    share = js // ranks
    moved[...] = jnp.swapaxes(w_ref[0].astype(jnp.float32), 0, 1).astype(w_ref.dtype)
    for distance, ref in enumerate(out_refs):
        first = lax.rem(lax.axis_index("rep") + distance, ranks) * share
        for j in range(share):
            ref[0, :, j * cols:(j + 1) * cols] = moved[first + j]


def integrals_by_j(integrals, ranks):
    nk, rows, js, cols = integrals.shape
    wide = js // ranks * cols
    return pl.pallas_call(
        functools.partial(by_j_body, ranks),
        out_shape=[jax.ShapeDtypeStruct((nk, rows, wide), integrals.dtype)] * ranks,
        grid=(nk,),
        in_specs=[pl.BlockSpec((1, rows, js, cols), lambda k: (k, 0, 0, 0))],
        out_specs=[pl.BlockSpec((1, rows, wide), lambda k: (k, 0, 0))] * ranks,
        scratch_shapes=[pltpu.VMEM((js, rows, cols), integrals.dtype)],
        compiler_params=params(16),
        cost_estimate=cost(0, 0),
        name="integrals_by_j",
    )(integrals)


def quarter_copies(refs, chosen, slot, quarter, sems):
    nk, rows, _ = refs[0].shape
    found = []
    for d, ref in enumerate(refs):
        place = pl.multiple_of(jnp.bitwise_xor(quarter, d) * rows, rows)
        found.append(
            pltpu.make_async_copy(
                ref, chosen.at[pl.ds(slot * nk, nk), pl.ds(place, rows), :], sems.at[4 * slot + d]
            )
        )
    return found


def product_body(plan, held, has_sum, is_held, quarter_ref, *refs):
    count = len(plan)
    pieces, refs = refs[:count], refs[count:]
    w_refs, refs = (refs[:1], refs[1:]) if is_held else (refs[:4 * (count + held)], refs[4 * (count + held):])
    sum_refs, refs = (refs[:1], refs[1:]) if has_sum else ((), refs)
    out_ref, refs = refs[0], refs[1:]
    held_ref, refs = (refs[0], refs[1:]) if held else (None, refs)
    lhs, total, piece_sems, *refs = refs
    chosen, w_sems, *held_sems = (w_refs[0], None) if is_held else refs
    width = w_refs[0].shape[2]
    ni, nk, step, cols = pieces[0].shape
    quarter = quarter_ref[0]

    def copies(slot):
        found = [pltpu.make_async_copy(pieces[slot], lhs.at[pl.ds(slot * ni, ni)], piece_sems.at[slot])]
        if not is_held:
            found += quarter_copies(w_refs[4 * slot:4 * slot + 4], chosen, slot, quarter, w_sems)
        return found

    waiting = [copies(slot) for slot in range(count)]
    later = []
    for n in range(held):
        first = 4 * (count + n)
        later += quarter_copies(w_refs[first:first + 4], held_ref, n, quarter, held_sems[0])
    for slot in range(min(AHEAD, count)):
        for copy in waiting[slot]:
            copy.start()
    for slot in range(count):
        for copy in waiting[slot]:
            copy.wait()
        if slot + AHEAD < count:
            for copy in waiting[slot + AHEAD]:
                copy.start()
        if slot == 0:
            for copy in later:
                copy.start()
        left = jnp.concatenate(
            [lhs[slot * ni:(slot + 1) * ni, k].reshape(ni * step, cols) for k in range(nk)], axis=1
        )
        right = chosen[slot * nk:(slot + 1) * nk].reshape(nk * cols, width)
        sums = jnp.dot(left, right, preferred_element_type=jnp.float32)
        if slot == 0:
            if has_sum:
                sums = sums + sum_refs[0][...]
        else:
            sums = sums + total[...]
        if slot < count - 1:
            total[...] = sums
        elif out_ref.dtype == jnp.float32:
            out_ref[...] = sums
        else:
            for j in range(width // cols):
                out_ref[:, j] = sums[:, j * cols:(j + 1) * cols].astype(out_ref.dtype).reshape(ni, step, cols)
    for copy in later:
        copy.wait()


def product(pieces, plan, chosen, quarter, sums=None, last=True, hold=()):
    ni, nk, step, cols = pieces[0].shape
    is_held = not isinstance(chosen, list)
    width = chosen.shape[2] if is_held else chosen[0][0].shape[2]
    js = width // cols
    w_parts = [chosen] if is_held else [part for block in (*plan, *hold) for part in chosen[block]]
    if sums is None:
        pieces = [pltpu.with_memory_space_constraint(piece, pltpu.HBM) for piece in pieces]
        w_parts = [pltpu.with_memory_space_constraint(part, pltpu.HBM) for part in w_parts]
    operands = [quarter.reshape(1), *pieces, *w_parts]
    in_specs = [pl.BlockSpec(memory_space=pltpu.SMEM)]
    in_specs += [pl.BlockSpec(memory_space=pl.ANY)] * (len(operands) - 1)
    if is_held:
        in_specs[-1] = pl.BlockSpec(memory_space=pltpu.VMEM)
        operands[-1] = pltpu.with_memory_space_constraint(chosen, pltpu.VMEM)
    if sums is not None:
        in_specs.append(pl.BlockSpec(memory_space=pltpu.VMEM))
        operands.append(sums)
    if last:
        out_shape = [jax.ShapeDtypeStruct((ni, js, step, cols), pieces[0].dtype)]
    else:
        out_shape = [jax.ShapeDtypeStruct((ni * step, width), jnp.float32)]
    if hold:
        out_shape.append(pltpu.VMEM((nk * len(hold), cols, width), pieces[0].dtype))
    count = len(plan)
    scratch = [
        pltpu.VMEM((ni * count, nk, step, cols), pieces[0].dtype),
        pltpu.VMEM((ni * step, width), jnp.float32),
        pltpu.SemaphoreType.DMA((count,)),
    ]
    if not is_held:
        scratch += [pltpu.VMEM((nk * count, cols, width), pieces[0].dtype), pltpu.SemaphoreType.DMA((4 * count,))]
    if hold:
        scratch.append(pltpu.SemaphoreType.DMA((4 * len(hold),)))
    return pl.pallas_call(
        functools.partial(product_body, plan, len(hold), sums is not None, is_held),
        out_shape=out_shape,
        in_specs=in_specs,
        out_specs=[pl.BlockSpec(memory_space=pltpu.VMEM)] * len(out_shape),
        scratch_shapes=scratch,
        compiler_params=params(VMEM_PRODUCT),
        cost_estimate=cost(0, 0),
        name="product",
    )(*operands)


def place_body(offset, xor_ref, part_ref, *refs):
    out_ref, sems = refs[-2:]
    irreps, _, step, _ = part_ref.shape
    copies = [
        pltpu.make_async_copy(
            part_ref.at[g],
            out_ref.at[:, jnp.bitwise_xor(g, xor_ref[0]), offset:offset + step],
            sems.at[g],
        )
        for g in range(irreps)
    ]
    for copy in copies:
        copy.start()
    for copy in copies:
        copy.wait()


def place_irreps(part, pair_xor, rows, offset, result):
    irreps, js, step, cols = part.shape
    operands = [pair_xor.reshape(1), part]
    aliases = {}
    if result is not None:
        aliases = {len(operands): 0}
        operands.append(result)
    return pl.pallas_call(
        functools.partial(place_body, offset),
        out_shape=jax.ShapeDtypeStruct((js, irreps, rows, cols), part.dtype),
        in_specs=[pl.BlockSpec(memory_space=pltpu.SMEM)]
        + [pl.BlockSpec(memory_space=pl.ANY)] * (len(operands) - 1),
        out_specs=pl.BlockSpec(memory_space=pl.ANY),
        scratch_shapes=[pltpu.SemaphoreType.DMA((irreps,))],
        input_output_aliases=aliases,
        compiler_params=params(16),
        cost_estimate=cost(0, 0),
        name="place_irreps",
    )(*operands)


def after(values, *earlier):
    return lax.optimization_barrier((values, earlier))[0]


def per_device(amplitudes, integrals, pair_irreps):
    quarters = lax.axis_size("ten") // IRREPS
    groups = [
        [g * quarters + (q ^ (g % 2 * quarters // 2)) for g in range(IRREPS)] for q in range(quarters)
    ]
    ranks = lax.axis_size("rep")
    quarter = lax.axis_index("ten") % quarters
    nk, rows = amplitudes.shape[1], amplitudes.shape[3]

    by_j = integrals_by_j(integrals, ranks)
    amplitudes, by_j = lax.optimization_barrier((amplitudes, by_j))
    amps = amplitudes.reshape(nk, IRREPS, rows, rows)
    by_group = order_amps(amps, pair_irreps, 0, STEPS[0])

    near = by_j[0]
    arrived = [near, shift_rep(by_j[1], 1), shift_rep(by_j[3], -1), shift_rep(by_j[2], 2)]
    by_group2 = order_amps(after(amps, arrived[1]), pair_irreps, STEPS[0], STEPS[1])
    arrived[2], by_group2 = lax.optimization_barrier((arrived[2], by_group2))
    zl = [flip_ten(part, 2) for part in arrived]
    core = [flip_ten(part, 1) for part in arrived]
    both = [flip_ten(part, 1) for part in zl]

    first = exchange_irreps(by_group, groups)
    first, near, core[1], core[2], zl[0], by_group2 = lax.optimization_barrier(
        (first, near, core[1], core[2], zl[0], by_group2)
    )
    core[0], both[0] = flip_ten(near, 1), flip_ten(zl[0], 1)
    by_group2, core[0], core[3] = lax.optimization_barrier((by_group2, core[0], core[3]))
    second = exchange_irreps(by_group2, groups)

    left, right = shift_rep(first, 1), shift_rep(first, -1)
    right2 = shift_rep(second, -1)
    left, right, zl[1] = lax.optimization_barrier((left, right, zl[1]))
    far = shift_rep(left, 1)
    both[1] = flip_ten(zl[1], 1)
    left2 = shift_rep(after(second, both[1]), 1)
    far2 = shift_rep(right2, -1)
    both[2], both[3] = flip_ten(zl[2], 1), flip_ten(zl[3], 1)
    chosen = [(arrived[n], core[n], zl[n], both[n]) for n in range(ranks)]

    (sums,) = product((first, left, right), (0, 1, 2), chosen, quarter, last=False)
    far, sums = lax.optimization_barrier((far, sums))
    (out,) = product((far,), (3,), chosen, quarter, sums=sums)
    back = exchange_irreps(out, groups)
    sums, held = product((second, right2), (0, 2), chosen, quarter, last=False, hold=(1, 3))
    left2, far2, sums, held = lax.optimization_barrier((left2, far2, sums, held))
    (out2,) = product((left2, far2), (1, 3), held, quarter, sums=sums)
    pair_xor = jnp.bitwise_xor(pair_irreps[0], pair_irreps[1])
    back, out2 = lax.optimization_barrier((back, out2))
    back2 = exchange_irreps(out2, groups)
    result = place_irreps(back, pair_xor, rows, 0, None)
    result = place_irreps(back2, pair_xor, rows, STEPS[0], result)
    return result.reshape(amplitudes.shape)


def solution(mesh):
    in_specs = (P("ten", "rep", None, None), P("rep", "ten", None, None), P())
    return jax.shard_map(
        per_device, mesh=mesh, in_specs=in_specs, out_specs=in_specs[0], check_vma=False
    )
```

```python
import functools

import jax
import jax.numpy as jnp
from jax import lax
from jax.experimental import pallas as pl
from jax.experimental.pallas import tpu as pltpu
from jax.sharding import PartitionSpec as P

IRREPS = 8
STEPS = (64, 64)
VMEM_PRODUCT = 24
AHEAD = 2
MIB = 1 << 20


def shift_rep(array, distance):
    n = lax.axis_size("rep")
    return lax.ppermute(array, "rep", [(s, (s + distance) % n) for s in range(n)])


def flip_ten(array, mask):
    return lax.ppermute(array, "ten", [(s, s ^ mask) for s in range(lax.axis_size("ten"))])


def exchange_irreps(array, groups):
    return lax.all_to_all(
        array, "ten", split_axis=0, concat_axis=0, axis_index_groups=groups, tiled=True
    )


def params(limit):
    return pltpu.CompilerParams(vmem_limit_bytes=limit * MIB)


def cost(flops, moved):
    return pl.CostEstimate(flops=0, bytes_accessed=0, transcendentals=0)


def order_body(offset, pair_ref, amps_ref, out_ref, sems):
    irreps, _, step, _ = out_ref.shape
    pair_xor = jnp.bitwise_xor(pair_ref[0], pair_ref[1])
    copies = [
        pltpu.make_async_copy(
            amps_ref.at[:, jnp.bitwise_xor(g, pair_xor), offset:offset + step],
            out_ref.at[g],
            sems.at[g],
        )
        for g in range(irreps)
    ]
    for copy in copies:
        copy.start()
    for copy in copies:
        copy.wait()


def order_amps(amps, pair_irreps, offset, step):
    nk, irreps, _, cols = amps.shape
    return pl.pallas_call(
        functools.partial(order_body, offset),
        out_shape=pltpu.VMEM((irreps, nk, step, cols), amps.dtype),
        in_specs=[pl.BlockSpec(memory_space=pltpu.SMEM), pl.BlockSpec(memory_space=pl.ANY)],
        out_specs=pl.BlockSpec(memory_space=pltpu.VMEM),
        scratch_shapes=[pltpu.SemaphoreType.DMA((irreps,))],
        compiler_params=params(16),
        cost_estimate=cost(0, 0),
        name="order_amps",
    )(pair_irreps, pltpu.with_memory_space_constraint(amps, pltpu.HBM))


def by_j_body(ranks, w_ref, *refs):
    out_refs, (held, moved, sems) = refs[:-3], refs[-3:]
    nk, rows, js, cols = w_ref.shape
    share = js // ranks
    step = pl.program_id(0)

    @pl.when(step == 0)
    def _():
        for k in range(nk):
            pltpu.make_async_copy(w_ref.at[k], held.at[k], sems.at[k]).start()

    pltpu.make_async_copy(w_ref.at[step], held.at[step], sems.at[step]).wait()
    moved[...] = jnp.swapaxes(held[step].astype(jnp.float32), 0, 1).astype(w_ref.dtype)
    for distance, ref in enumerate(out_refs):
        first = lax.rem(lax.axis_index("rep") + distance, ranks) * share
        for j in range(share):
            ref[0, :, j * cols:(j + 1) * cols] = moved[first + j]


def integrals_by_j(integrals, ranks):
    nk, rows, js, cols = integrals.shape
    wide = js // ranks * cols
    return pl.pallas_call(
        functools.partial(by_j_body, ranks),
        out_shape=[jax.ShapeDtypeStruct((nk, rows, wide), integrals.dtype)] * ranks,
        grid=(nk,),
        in_specs=[pl.BlockSpec(memory_space=pl.ANY)],
        out_specs=[pl.BlockSpec((1, rows, wide), lambda k: (k, 0, 0))] * ranks,
        scratch_shapes=[
            pltpu.VMEM((nk, rows, js, cols), integrals.dtype),
            pltpu.VMEM((js, rows, cols), integrals.dtype),
            pltpu.SemaphoreType.DMA((nk,)),
        ],
        compiler_params=params(16),
        cost_estimate=cost(0, 0),
        name="integrals_by_j",
    )(pltpu.with_memory_space_constraint(integrals, pltpu.HBM))


def quarter_copies(refs, chosen, slot, quarter, sems):
    nk, rows, _ = refs[0].shape
    found = []
    for d, ref in enumerate(refs):
        place = pl.multiple_of(jnp.bitwise_xor(quarter, d) * rows, rows)
        found.append(
            pltpu.make_async_copy(
                ref, chosen.at[pl.ds(slot * nk, nk), pl.ds(place, rows), :], sems.at[4 * slot + d]
            )
        )
    return found


def product_body(plan, held, has_sum, is_held, quarter_ref, *refs):
    count = len(plan)
    pieces, refs = refs[:count], refs[count:]
    w_refs, refs = (refs[:1], refs[1:]) if is_held else (refs[:4 * (count + held)], refs[4 * (count + held):])
    sum_refs, refs = (refs[:1], refs[1:]) if has_sum else ((), refs)
    out_ref, refs = refs[0], refs[1:]
    held_ref, refs = (refs[0], refs[1:]) if held else (None, refs)
    lhs, total, piece_sems, *refs = refs
    chosen, w_sems, *held_sems = (w_refs[0], None) if is_held else refs
    width = w_refs[0].shape[2]
    ni, nk, step, cols = pieces[0].shape
    quarter = quarter_ref[0]

    def copies(slot):
        found = [pltpu.make_async_copy(pieces[slot], lhs.at[pl.ds(slot * ni, ni)], piece_sems.at[slot])]
        if not is_held:
            found += quarter_copies(w_refs[4 * slot:4 * slot + 4], chosen, slot, quarter, w_sems)
        return found

    waiting = [copies(slot) for slot in range(count)]
    later = []
    for n in range(held):
        first = 4 * (count + n)
        later += quarter_copies(w_refs[first:first + 4], held_ref, n, quarter, held_sems[0])
    for slot in range(min(AHEAD, count)):
        for copy in waiting[slot]:
            copy.start()
    for slot in range(count):
        for copy in waiting[slot]:
            copy.wait()
        if slot + AHEAD < count:
            for copy in waiting[slot + AHEAD]:
                copy.start()
        if slot == 0:
            for copy in later:
                copy.start()
        left = jnp.concatenate(
            [lhs[slot * ni:(slot + 1) * ni, k].reshape(ni * step, cols) for k in range(nk)], axis=1
        )
        right = chosen[slot * nk:(slot + 1) * nk].reshape(nk * cols, width)
        sums = jnp.dot(left, right, preferred_element_type=jnp.float32)
        if slot == 0:
            if has_sum:
                sums = sums + sum_refs[0][...]
        else:
            sums = sums + total[...]
        if slot < count - 1:
            total[...] = sums
        elif out_ref.dtype == jnp.float32:
            out_ref[...] = sums
        else:
            for j in range(width // cols):
                out_ref[:, j] = sums[:, j * cols:(j + 1) * cols].astype(out_ref.dtype).reshape(ni, step, cols)
    for copy in later:
        copy.wait()


def product(pieces, plan, chosen, quarter, sums=None, last=True, hold=()):
    ni, nk, step, cols = pieces[0].shape
    is_held = not isinstance(chosen, list)
    width = chosen.shape[2] if is_held else chosen[0][0].shape[2]
    js = width // cols
    w_parts = [chosen] if is_held else [part for block in (*plan, *hold) for part in chosen[block]]
    if sums is None:
        pieces = [pltpu.with_memory_space_constraint(piece, pltpu.HBM) for piece in pieces]
        w_parts = [pltpu.with_memory_space_constraint(part, pltpu.HBM) for part in w_parts]
    operands = [quarter.reshape(1), *pieces, *w_parts]
    in_specs = [pl.BlockSpec(memory_space=pltpu.SMEM)]
    in_specs += [pl.BlockSpec(memory_space=pl.ANY)] * (len(operands) - 1)
    if is_held:
        in_specs[-1] = pl.BlockSpec(memory_space=pltpu.VMEM)
        operands[-1] = pltpu.with_memory_space_constraint(chosen, pltpu.VMEM)
    if sums is not None:
        in_specs.append(pl.BlockSpec(memory_space=pltpu.VMEM))
        operands.append(sums)
    if last:
        out_shape = [jax.ShapeDtypeStruct((ni, js, step, cols), pieces[0].dtype)]
    else:
        out_shape = [jax.ShapeDtypeStruct((ni * step, width), jnp.float32)]
    if hold:
        out_shape.append(pltpu.VMEM((nk * len(hold), cols, width), pieces[0].dtype))
    count = len(plan)
    scratch = [
        pltpu.VMEM((ni * count, nk, step, cols), pieces[0].dtype),
        pltpu.VMEM((ni * step, width), jnp.float32),
        pltpu.SemaphoreType.DMA((count,)),
    ]
    if not is_held:
        scratch += [pltpu.VMEM((nk * count, cols, width), pieces[0].dtype), pltpu.SemaphoreType.DMA((4 * count,))]
    if hold:
        scratch.append(pltpu.SemaphoreType.DMA((4 * len(hold),)))
    return pl.pallas_call(
        functools.partial(product_body, plan, len(hold), sums is not None, is_held),
        out_shape=out_shape,
        in_specs=in_specs,
        out_specs=[pl.BlockSpec(memory_space=pltpu.VMEM)] * len(out_shape),
        scratch_shapes=scratch,
        compiler_params=params(VMEM_PRODUCT),
        cost_estimate=cost(0, 0),
        name="product",
    )(*operands)


def place_body(offset, xor_ref, part_ref, *refs):
    out_ref, sems = refs[-2:]
    irreps, _, step, _ = part_ref.shape
    copies = [
        pltpu.make_async_copy(
            part_ref.at[g],
            out_ref.at[:, jnp.bitwise_xor(g, xor_ref[0]), offset:offset + step],
            sems.at[g],
        )
        for g in range(irreps)
    ]
    for copy in copies:
        copy.start()
    for copy in copies:
        copy.wait()


def place_irreps(part, pair_xor, rows, offset, result):
    irreps, js, step, cols = part.shape
    operands = [pair_xor.reshape(1), part]
    aliases = {}
    if result is not None:
        aliases = {len(operands): 0}
        operands.append(result)
    return pl.pallas_call(
        functools.partial(place_body, offset),
        out_shape=jax.ShapeDtypeStruct((js, irreps, rows, cols), part.dtype),
        in_specs=[pl.BlockSpec(memory_space=pltpu.SMEM)]
        + [pl.BlockSpec(memory_space=pl.ANY)] * (len(operands) - 1),
        out_specs=pl.BlockSpec(memory_space=pl.ANY),
        scratch_shapes=[pltpu.SemaphoreType.DMA((irreps,))],
        input_output_aliases=aliases,
        compiler_params=params(16),
        cost_estimate=cost(0, 0),
        name="place_irreps",
    )(*operands)


def after(values, *earlier):
    return lax.optimization_barrier((values, earlier))[0]


def per_device(amplitudes, integrals, pair_irreps):
    quarters = lax.axis_size("ten") // IRREPS
    groups = [
        [g * quarters + (q ^ (g % 2 * quarters // 2)) for g in range(IRREPS)] for q in range(quarters)
    ]
    ranks = lax.axis_size("rep")
    quarter = lax.axis_index("ten") % quarters
    nk, rows = amplitudes.shape[1], amplitudes.shape[3]

    by_j = integrals_by_j(integrals, ranks)
    amplitudes, by_j = lax.optimization_barrier((amplitudes, by_j))
    amps = amplitudes.reshape(nk, IRREPS, rows, rows)
    by_group = order_amps(amps, pair_irreps, 0, STEPS[0])

    near = by_j[0]
    arrived = [near, shift_rep(by_j[1], 1), shift_rep(by_j[3], -1), shift_rep(by_j[2], 2)]
    by_group2 = order_amps(after(amps, arrived[1]), pair_irreps, STEPS[0], STEPS[1])
    arrived[2], by_group2 = lax.optimization_barrier((arrived[2], by_group2))
    zl = [flip_ten(part, 2) for part in arrived]
    core = [flip_ten(part, 1) for part in arrived]
    both = [flip_ten(part, 1) for part in zl]

    first = exchange_irreps(by_group, groups)
    first, near, core[1], core[2], zl[0], by_group2 = lax.optimization_barrier(
        (first, near, core[1], core[2], zl[0], by_group2)
    )
    core[0], both[0] = flip_ten(near, 1), flip_ten(zl[0], 1)
    by_group2, core[0], core[3] = lax.optimization_barrier((by_group2, core[0], core[3]))
    second = exchange_irreps(by_group2, groups)

    left, right = shift_rep(first, 1), shift_rep(first, -1)
    right2 = shift_rep(second, -1)
    left, right, zl[1] = lax.optimization_barrier((left, right, zl[1]))
    far = shift_rep(left, 1)
    both[1] = flip_ten(zl[1], 1)
    left2 = shift_rep(after(second, both[1]), 1)
    far2 = shift_rep(right2, -1)
    both[2], both[3] = flip_ten(zl[2], 1), flip_ten(zl[3], 1)
    chosen = [(arrived[n], core[n], zl[n], both[n]) for n in range(ranks)]

    (sums,) = product((first, left, right), (0, 1, 2), chosen, quarter, last=False)
    far, sums = lax.optimization_barrier((far, sums))
    (out,) = product((far,), (3,), chosen, quarter, sums=sums)
    back = exchange_irreps(out, groups)
    sums, held = product((second, right2), (0, 2), chosen, quarter, last=False, hold=(1, 3))
    left2, far2, sums, held = lax.optimization_barrier((left2, far2, sums, held))
    (out2,) = product((left2, far2), (1, 3), held, quarter, sums=sums)
    pair_xor = jnp.bitwise_xor(pair_irreps[0], pair_irreps[1])
    back, out2 = lax.optimization_barrier((back, out2))
    back2 = exchange_irreps(out2, groups)
    result = place_irreps(back, pair_xor, rows, 0, None)
    result = place_irreps(back2, pair_xor, rows, STEPS[0], result)
    return result.reshape(amplitudes.shape)


def solution(mesh):
    in_specs = (P("ten", "rep", None, None), P("rep", "ten", None, None), P())
    return jax.shard_map(
        per_device, mesh=mesh, in_specs=in_specs, out_specs=in_specs[0], check_vma=False
    )
```

```python
import functools

import jax
import jax.numpy as jnp
from jax import lax
from jax.experimental import pallas as pl
from jax.experimental.pallas import tpu as pltpu
from jax.sharding import PartitionSpec as P

IRREPS = 8
STEPS = (64, 64)
VMEM_PRODUCT = 24
AHEAD = 2
MIB = 1 << 20


def shift_rep(array, distance):
    n = lax.axis_size("rep")
    return lax.ppermute(array, "rep", [(s, (s + distance) % n) for s in range(n)])


def flip_ten(array, mask):
    return lax.ppermute(array, "ten", [(s, s ^ mask) for s in range(lax.axis_size("ten"))])


def exchange_irreps(array, groups):
    return lax.all_to_all(
        array, "ten", split_axis=0, concat_axis=0, axis_index_groups=groups, tiled=True
    )


def params(limit):
    return pltpu.CompilerParams(vmem_limit_bytes=limit * MIB)


def cost(flops, moved):
    return pl.CostEstimate(flops=0, bytes_accessed=0, transcendentals=0)


def order_body(offset, pair_ref, amps_ref, out_ref, sems):
    irreps, _, step, _ = out_ref.shape
    pair_xor = jnp.bitwise_xor(pair_ref[0], pair_ref[1])
    copies = [
        pltpu.make_async_copy(
            amps_ref.at[:, jnp.bitwise_xor(g, pair_xor), offset:offset + step],
            out_ref.at[g],
            sems.at[g],
        )
        for g in range(irreps)
    ]
    for copy in copies:
        copy.start()
    for copy in copies:
        copy.wait()


def order_amps(amps, pair_irreps, offset, step):
    nk, irreps, _, cols = amps.shape
    return pl.pallas_call(
        functools.partial(order_body, offset),
        out_shape=pltpu.VMEM((irreps, nk, step, cols), amps.dtype),
        in_specs=[pl.BlockSpec(memory_space=pltpu.SMEM), pl.BlockSpec(memory_space=pl.ANY)],
        out_specs=pl.BlockSpec(memory_space=pltpu.VMEM),
        scratch_shapes=[pltpu.SemaphoreType.DMA((irreps,))],
        compiler_params=params(16),
        cost_estimate=cost(0, 0),
        name="order_amps",
    )(pair_irreps, pltpu.with_memory_space_constraint(amps, pltpu.HBM))


def by_j_body(ranks, w_ref, *refs):
    out_refs, (held, moved, sems) = refs[:-3], refs[-3:]
    nk, rows, js, cols = w_ref.shape
    share = js // ranks
    step = pl.program_id(0)

    @pl.when(step == 0)
    def _():
        for k in range(nk):
            pltpu.make_async_copy(w_ref.at[k], held.at[k], sems.at[k]).start()

    pltpu.make_async_copy(w_ref.at[step], held.at[step], sems.at[step]).wait()
    moved[...] = jnp.swapaxes(held[step].astype(jnp.float32), 0, 1).astype(w_ref.dtype)
    for distance, ref in enumerate(out_refs):
        first = lax.rem(lax.axis_index("rep") + distance, ranks) * share
        for j in range(share):
            ref[0, :, j * cols:(j + 1) * cols] = moved[first + j]


def integrals_by_j(integrals, ranks):
    nk, rows, js, cols = integrals.shape
    wide = js // ranks * cols
    return pl.pallas_call(
        functools.partial(by_j_body, ranks),
        out_shape=[jax.ShapeDtypeStruct((nk, rows, wide), integrals.dtype)] * ranks,
        grid=(nk,),
        in_specs=[pl.BlockSpec(memory_space=pl.ANY)],
        out_specs=[pl.BlockSpec((1, rows, wide), lambda k: (k, 0, 0))] * ranks,
        scratch_shapes=[
            pltpu.VMEM((nk, rows, js, cols), integrals.dtype),
            pltpu.VMEM((js, rows, cols), integrals.dtype),
            pltpu.SemaphoreType.DMA((nk,)),
        ],
        compiler_params=params(16),
        cost_estimate=cost(0, 0),
        name="integrals_by_j",
    )(pltpu.with_memory_space_constraint(integrals, pltpu.HBM))


def quarter_copies(refs, chosen, slot, quarter, sems):
    nk, rows, _ = refs[0].shape
    found = []
    for d, ref in enumerate(refs):
        place = pl.multiple_of(jnp.bitwise_xor(quarter, d) * rows, rows)
        found.append(
            pltpu.make_async_copy(
                ref, chosen.at[pl.ds(slot * nk, nk), pl.ds(place, rows), :], sems.at[4 * slot + d]
            )
        )
    return found


def product_body(plan, held, has_sum, is_held, quarter_ref, *refs):
    count = len(plan)
    pieces, refs = refs[:count], refs[count:]
    w_refs, refs = (refs[:1], refs[1:]) if is_held else (refs[:4 * (count + held)], refs[4 * (count + held):])
    sum_refs, refs = (refs[:1], refs[1:]) if has_sum else ((), refs)
    out_ref, refs = refs[0], refs[1:]
    held_ref, refs = (refs[0], refs[1:]) if held else (None, refs)
    lhs, total, piece_sems, *refs = refs
    if out_ref.dtype != jnp.float32:
        *refs, staged, out_sems = refs
    chosen, w_sems, *held_sems = (w_refs[0], None) if is_held else refs
    width = w_refs[0].shape[2]
    ni, nk, step, cols = pieces[0].shape
    quarter = quarter_ref[0]

    def copies(slot):
        found = [pltpu.make_async_copy(pieces[slot], lhs.at[pl.ds(slot * ni, ni)], piece_sems.at[slot])]
        if not is_held:
            found += quarter_copies(w_refs[4 * slot:4 * slot + 4], chosen, slot, quarter, w_sems)
        return found

    waiting = [copies(slot) for slot in range(count)]
    later = []
    for n in range(held):
        first = 4 * (count + n)
        later += quarter_copies(w_refs[first:first + 4], held_ref, n, quarter, held_sems[0])
    for slot in range(min(AHEAD, count)):
        for copy in waiting[slot]:
            copy.start()
    for slot in range(count):
        for copy in waiting[slot]:
            copy.wait()
        if slot + AHEAD < count:
            for copy in waiting[slot + AHEAD]:
                copy.start()
        if slot == 0:
            for copy in later:
                copy.start()
        left = jnp.concatenate(
            [lhs[slot * ni:(slot + 1) * ni, k].reshape(ni * step, cols) for k in range(nk)], axis=1
        )
        right = chosen[slot * nk:(slot + 1) * nk].reshape(nk * cols, width)
        if slot == count - 1 and out_ref.dtype != jnp.float32:
            js = out_ref.shape[1] // 2
            leaving = []
            for n in range(2):
                here = slice(n * js * cols, (n + 1) * js * cols)
                sums = jnp.dot(left, right[:, here], preferred_element_type=jnp.float32)
                sums = sums + (sum_refs[0] if slot == 0 else total)[:, here]
                for j in range(js):
                    part = sums[:, j * cols:(j + 1) * cols].astype(out_ref.dtype)
                    staged[:, n * js + j] = part.reshape(ni, step, cols)
                place = pl.ds(n * js, js)
                leaving.append(
                    pltpu.make_async_copy(staged.at[:, place], out_ref.at[:, place], out_sems.at[n])
                )
                leaving[-1].start()
            for copy in leaving:
                copy.wait()
            continue
        sums = jnp.dot(left, right, preferred_element_type=jnp.float32)
        if slot == 0:
            if has_sum:
                sums = sums + sum_refs[0][...]
        else:
            sums = sums + total[...]
        if slot < count - 1:
            total[...] = sums
        else:
            out_ref[...] = sums
    for copy in later:
        copy.wait()


def product(pieces, plan, chosen, quarter, sums=None, last=True, hold=()):
    ni, nk, step, cols = pieces[0].shape
    is_held = not isinstance(chosen, list)
    width = chosen.shape[2] if is_held else chosen[0][0].shape[2]
    js = width // cols
    w_parts = [chosen] if is_held else [part for block in (*plan, *hold) for part in chosen[block]]
    if sums is None:
        pieces = [pltpu.with_memory_space_constraint(piece, pltpu.HBM) for piece in pieces]
        w_parts = [pltpu.with_memory_space_constraint(part, pltpu.HBM) for part in w_parts]
    operands = [quarter.reshape(1), *pieces, *w_parts]
    in_specs = [pl.BlockSpec(memory_space=pltpu.SMEM)]
    in_specs += [pl.BlockSpec(memory_space=pl.ANY)] * (len(operands) - 1)
    if is_held:
        in_specs[-1] = pl.BlockSpec(memory_space=pltpu.VMEM)
        operands[-1] = pltpu.with_memory_space_constraint(chosen, pltpu.VMEM)
    if sums is not None:
        in_specs.append(pl.BlockSpec(memory_space=pltpu.VMEM))
        operands.append(sums)
    if last:
        out_shape = [jax.ShapeDtypeStruct((ni, js, step, cols), pieces[0].dtype)]
    else:
        out_shape = [jax.ShapeDtypeStruct((ni * step, width), jnp.float32)]
    if hold:
        out_shape.append(pltpu.VMEM((nk * len(hold), cols, width), pieces[0].dtype))
    count = len(plan)
    scratch = [
        pltpu.VMEM((ni * count, nk, step, cols), pieces[0].dtype),
        pltpu.VMEM((ni * step, width), jnp.float32),
        pltpu.SemaphoreType.DMA((count,)),
    ]
    if not is_held:
        scratch += [pltpu.VMEM((nk * count, cols, width), pieces[0].dtype), pltpu.SemaphoreType.DMA((4 * count,))]
    if hold:
        scratch.append(pltpu.SemaphoreType.DMA((4 * len(hold),)))
    if last:
        scratch += [pltpu.VMEM((ni, js, step, cols), pieces[0].dtype), pltpu.SemaphoreType.DMA((2,))]
    return pl.pallas_call(
        functools.partial(product_body, plan, len(hold), sums is not None, is_held),
        out_shape=out_shape,
        in_specs=in_specs,
        out_specs=[pl.BlockSpec(memory_space=pl.ANY if last else pltpu.VMEM)] * len(out_shape),
        scratch_shapes=scratch,
        compiler_params=params(VMEM_PRODUCT),
        cost_estimate=cost(0, 0),
        name="product",
    )(*operands)


def place_body(offset, xor_ref, part_ref, *refs):
    out_ref, sems = refs[-2:]
    irreps, _, step, _ = part_ref.shape
    copies = [
        pltpu.make_async_copy(
            part_ref.at[g],
            out_ref.at[:, jnp.bitwise_xor(g, xor_ref[0]), offset:offset + step],
            sems.at[g],
        )
        for g in range(irreps)
    ]
    for copy in copies:
        copy.start()
    for copy in copies:
        copy.wait()


def place_irreps(part, pair_xor, rows, offset, result):
    irreps, js, step, cols = part.shape
    operands = [pair_xor.reshape(1), part]
    aliases = {}
    if result is not None:
        aliases = {len(operands): 0}
        operands.append(result)
    return pl.pallas_call(
        functools.partial(place_body, offset),
        out_shape=jax.ShapeDtypeStruct((js, irreps, rows, cols), part.dtype),
        in_specs=[pl.BlockSpec(memory_space=pltpu.SMEM)]
        + [pl.BlockSpec(memory_space=pl.ANY)] * (len(operands) - 1),
        out_specs=pl.BlockSpec(memory_space=pl.ANY),
        scratch_shapes=[pltpu.SemaphoreType.DMA((irreps,))],
        input_output_aliases=aliases,
        compiler_params=params(16),
        cost_estimate=cost(0, 0),
        name="place_irreps",
    )(*operands)


def after(values, *earlier):
    return lax.optimization_barrier((values, earlier))[0]


def per_device(amplitudes, integrals, pair_irreps):
    quarters = lax.axis_size("ten") // IRREPS
    groups = [
        [g * quarters + (q ^ (g % 2 * quarters // 2)) for g in range(IRREPS)] for q in range(quarters)
    ]
    ranks = lax.axis_size("rep")
    quarter = lax.axis_index("ten") % quarters
    nk, rows = amplitudes.shape[1], amplitudes.shape[3]

    by_j = integrals_by_j(integrals, ranks)
    amplitudes, by_j = lax.optimization_barrier((amplitudes, by_j))
    amps = amplitudes.reshape(nk, IRREPS, rows, rows)
    by_group = order_amps(amps, pair_irreps, 0, STEPS[0])

    near = by_j[0]
    arrived = [near, shift_rep(by_j[1], 1), shift_rep(by_j[3], -1), shift_rep(by_j[2], 2)]
    by_group2 = order_amps(after(amps, arrived[1]), pair_irreps, STEPS[0], STEPS[1])
    arrived[2], by_group2 = lax.optimization_barrier((arrived[2], by_group2))
    zl = [flip_ten(part, 2) for part in arrived]
    core = [flip_ten(part, 1) for part in arrived]
    both = [flip_ten(part, 1) for part in zl]

    first = exchange_irreps(by_group, groups)
    first, near, core[1], core[2], zl[0], by_group2 = lax.optimization_barrier(
        (first, near, core[1], core[2], zl[0], by_group2)
    )
    core[0], both[0] = flip_ten(near, 1), flip_ten(zl[0], 1)
    by_group2, core[0], core[3] = lax.optimization_barrier((by_group2, core[0], core[3]))
    second = exchange_irreps(by_group2, groups)

    left, right = shift_rep(first, 1), shift_rep(first, -1)
    right2 = shift_rep(second, -1)
    left, right, zl[1] = lax.optimization_barrier((left, right, zl[1]))
    far = shift_rep(left, 1)
    both[1] = flip_ten(zl[1], 1)
    left2 = shift_rep(after(second, both[1]), 1)
    far2 = shift_rep(right2, -1)
    both[2], both[3] = flip_ten(zl[2], 1), flip_ten(zl[3], 1)
    chosen = [(arrived[n], core[n], zl[n], both[n]) for n in range(ranks)]

    (sums,) = product((first, left, right), (0, 1, 2), chosen, quarter, last=False)
    far, sums = lax.optimization_barrier((far, sums))
    (out,) = product((far,), (3,), chosen, quarter, sums=sums)
    back = exchange_irreps(out, groups)
    sums, held = product((second, right2), (0, 2), chosen, quarter, last=False, hold=(1, 3))
    left2, far2, sums, held = lax.optimization_barrier((left2, far2, sums, held))
    (out2,) = product((left2, far2), (1, 3), held, quarter, sums=sums)
    pair_xor = jnp.bitwise_xor(pair_irreps[0], pair_irreps[1])
    back, out2 = lax.optimization_barrier((back, out2))
    back2 = exchange_irreps(out2, groups)
    result = place_irreps(back, pair_xor, rows, 0, None)
    result = place_irreps(back2, pair_xor, rows, STEPS[0], result)
    return result.reshape(amplitudes.shape)


def solution(mesh):
    in_specs = (P("ten", "rep", None, None), P("rep", "ten", None, None), P())
    return jax.shard_map(
        per_device, mesh=mesh, in_specs=in_specs, out_specs=in_specs[0], check_vma=False
    )
```

```python
import functools

import jax
import jax.numpy as jnp
from jax import lax
from jax.experimental import pallas as pl
from jax.experimental.pallas import tpu as pltpu
from jax.sharding import PartitionSpec as P

IRREPS = 8
STEPS = (64, 64)
VMEM_PRODUCT = 24
AHEAD = 2
MIB = 1 << 20


def shift_rep(array, distance):
    n = lax.axis_size("rep")
    return lax.ppermute(array, "rep", [(s, (s + distance) % n) for s in range(n)])


def flip_ten(array, mask):
    return lax.ppermute(array, "ten", [(s, s ^ mask) for s in range(lax.axis_size("ten"))])


def exchange_irreps(array, groups):
    return lax.all_to_all(
        array, "ten", split_axis=0, concat_axis=0, axis_index_groups=groups, tiled=True
    )


def params(limit):
    return pltpu.CompilerParams(vmem_limit_bytes=limit * MIB)


def cost(flops, moved):
    return pl.CostEstimate(flops=0, bytes_accessed=0, transcendentals=0)


def order_body(offset, pair_ref, amps_ref, out_ref, held, in_sems, out_sems):
    irreps, _, step, _ = held.shape
    pair_xor = jnp.bitwise_xor(pair_ref[0], pair_ref[1])
    arriving = [
        pltpu.make_async_copy(
            amps_ref.at[:, jnp.bitwise_xor(g, pair_xor), offset:offset + step], held.at[g], in_sems.at[g]
        )
        for g in range(irreps)
    ]
    leaving = [pltpu.make_async_copy(held.at[g], out_ref.at[g], out_sems.at[g]) for g in range(irreps)]
    for copy in arriving:
        copy.start()
    for g in range(irreps):
        arriving[g].wait()
        leaving[g].start()
    for copy in leaving:
        copy.wait()


def order_amps(amps, pair_irreps, offset, step):
    nk, irreps, _, cols = amps.shape
    return pl.pallas_call(
        functools.partial(order_body, offset),
        out_shape=jax.ShapeDtypeStruct((irreps, nk, step, cols), amps.dtype),
        in_specs=[pl.BlockSpec(memory_space=pltpu.SMEM), pl.BlockSpec(memory_space=pl.ANY)],
        out_specs=pl.BlockSpec(memory_space=pl.ANY),
        scratch_shapes=[
            pltpu.VMEM((irreps, nk, step, cols), amps.dtype),
            pltpu.SemaphoreType.DMA((irreps,)),
            pltpu.SemaphoreType.DMA((irreps,)),
        ],
        compiler_params=params(16),
        cost_estimate=cost(0, 0),
        name="order_amps",
    )(pair_irreps, pltpu.with_memory_space_constraint(amps, pltpu.HBM))


def by_j_body(ranks, w_ref, *refs):
    out_refs, (held, moved, sems) = refs[:-3], refs[-3:]
    nk, rows, js, cols = w_ref.shape
    share = js // ranks
    step = pl.program_id(0)

    @pl.when(step == 0)
    def _():
        for k in range(nk):
            pltpu.make_async_copy(w_ref.at[k], held.at[k], sems.at[k]).start()

    pltpu.make_async_copy(w_ref.at[step], held.at[step], sems.at[step]).wait()
    moved[...] = jnp.swapaxes(held[step].astype(jnp.float32), 0, 1).astype(w_ref.dtype)
    for distance, ref in enumerate(out_refs):
        first = lax.rem(lax.axis_index("rep") + distance, ranks) * share
        for j in range(share):
            ref[0, :, j * cols:(j + 1) * cols] = moved[first + j]


def integrals_by_j(integrals, ranks):
    nk, rows, js, cols = integrals.shape
    wide = js // ranks * cols
    return pl.pallas_call(
        functools.partial(by_j_body, ranks),
        out_shape=[jax.ShapeDtypeStruct((nk, rows, wide), integrals.dtype)] * ranks,
        grid=(nk,),
        in_specs=[pl.BlockSpec(memory_space=pl.ANY)],
        out_specs=[pl.BlockSpec((1, rows, wide), lambda k: (k, 0, 0))] * ranks,
        scratch_shapes=[
            pltpu.VMEM((nk, rows, js, cols), integrals.dtype),
            pltpu.VMEM((js, rows, cols), integrals.dtype),
            pltpu.SemaphoreType.DMA((nk,)),
        ],
        compiler_params=params(16),
        cost_estimate=cost(0, 0),
        name="integrals_by_j",
    )(pltpu.with_memory_space_constraint(integrals, pltpu.HBM))


def quarter_copies(refs, chosen, slot, quarter, sems):
    nk, rows, _ = refs[0].shape
    found = []
    for d, ref in enumerate(refs):
        place = pl.multiple_of(jnp.bitwise_xor(quarter, d) * rows, rows)
        found.append(
            pltpu.make_async_copy(
                ref, chosen.at[pl.ds(slot * nk, nk), pl.ds(place, rows), :], sems.at[4 * slot + d]
            )
        )
    return found


def product_body(plan, held, has_sum, is_held, quarter_ref, *refs):
    count = len(plan)
    pieces, refs = refs[:count], refs[count:]
    w_refs, refs = (refs[:1], refs[1:]) if is_held else (refs[:4 * (count + held)], refs[4 * (count + held):])
    sum_refs, refs = (refs[:1], refs[1:]) if has_sum else ((), refs)
    out_ref, refs = refs[0], refs[1:]
    held_ref, refs = (refs[0], refs[1:]) if held else (None, refs)
    lhs, total, piece_sems, *refs = refs
    chosen, w_sems, *held_sems = (w_refs[0], None) if is_held else refs
    width = w_refs[0].shape[2]
    ni, nk, step, cols = pieces[0].shape
    quarter = quarter_ref[0]

    def copies(slot):
        found = [pltpu.make_async_copy(pieces[slot], lhs.at[pl.ds(slot * ni, ni)], piece_sems.at[slot])]
        if not is_held:
            found += quarter_copies(w_refs[4 * slot:4 * slot + 4], chosen, slot, quarter, w_sems)
        return found

    waiting = [copies(slot) for slot in range(count)]
    later = []
    for n in range(held):
        first = 4 * (count + n)
        later += quarter_copies(w_refs[first:first + 4], held_ref, n, quarter, held_sems[0])
    for slot in range(min(AHEAD, count)):
        for copy in waiting[slot]:
            copy.start()
    for slot in range(count):
        for copy in waiting[slot]:
            copy.wait()
        if slot + AHEAD < count:
            for copy in waiting[slot + AHEAD]:
                copy.start()
        if slot == 0:
            for copy in later:
                copy.start()
        left = jnp.concatenate(
            [lhs[slot * ni:(slot + 1) * ni, k].reshape(ni * step, cols) for k in range(nk)], axis=1
        )
        right = chosen[slot * nk:(slot + 1) * nk].reshape(nk * cols, width)
        sums = jnp.dot(left, right, preferred_element_type=jnp.float32)
        if slot == 0:
            if has_sum:
                sums = sums + sum_refs[0][...]
        else:
            sums = sums + total[...]
        if slot < count - 1:
            total[...] = sums
        elif out_ref.dtype == jnp.float32:
            out_ref[...] = sums
        else:
            for j in range(width // cols):
                out_ref[:, j] = sums[:, j * cols:(j + 1) * cols].astype(out_ref.dtype).reshape(ni, step, cols)
    for copy in later:
        copy.wait()


def product(pieces, plan, chosen, quarter, sums=None, last=True, hold=()):
    ni, nk, step, cols = pieces[0].shape
    is_held = not isinstance(chosen, list)
    width = chosen.shape[2] if is_held else chosen[0][0].shape[2]
    js = width // cols
    w_parts = [chosen] if is_held else [part for block in (*plan, *hold) for part in chosen[block]]
    if sums is None:
        pieces = [pltpu.with_memory_space_constraint(piece, pltpu.HBM) for piece in pieces]
        w_parts = [pltpu.with_memory_space_constraint(part, pltpu.HBM) for part in w_parts]
    operands = [quarter.reshape(1), *pieces, *w_parts]
    in_specs = [pl.BlockSpec(memory_space=pltpu.SMEM)]
    in_specs += [pl.BlockSpec(memory_space=pl.ANY)] * (len(operands) - 1)
    if is_held:
        in_specs[-1] = pl.BlockSpec(memory_space=pltpu.VMEM)
        operands[-1] = pltpu.with_memory_space_constraint(chosen, pltpu.VMEM)
    if sums is not None:
        in_specs.append(pl.BlockSpec(memory_space=pltpu.VMEM))
        operands.append(sums)
    if last:
        out_shape = [jax.ShapeDtypeStruct((ni, js, step, cols), pieces[0].dtype)]
    else:
        out_shape = [jax.ShapeDtypeStruct((ni * step, width), jnp.float32)]
    if hold:
        out_shape.append(pltpu.VMEM((nk * len(hold), cols, width), pieces[0].dtype))
    count = len(plan)
    scratch = [
        pltpu.VMEM((ni * count, nk, step, cols), pieces[0].dtype),
        pltpu.VMEM((ni * step, width), jnp.float32),
        pltpu.SemaphoreType.DMA((count,)),
    ]
    if not is_held:
        scratch += [pltpu.VMEM((nk * count, cols, width), pieces[0].dtype), pltpu.SemaphoreType.DMA((4 * count,))]
    if hold:
        scratch.append(pltpu.SemaphoreType.DMA((4 * len(hold),)))
    return pl.pallas_call(
        functools.partial(product_body, plan, len(hold), sums is not None, is_held),
        out_shape=out_shape,
        in_specs=in_specs,
        out_specs=[pl.BlockSpec(memory_space=pltpu.VMEM)] * len(out_shape),
        scratch_shapes=scratch,
        compiler_params=params(VMEM_PRODUCT),
        cost_estimate=cost(0, 0),
        name="product",
    )(*operands)


def place_body(offset, xor_ref, part_ref, *refs):
    out_ref, sems = refs[-2:]
    irreps, _, step, _ = part_ref.shape
    copies = [
        pltpu.make_async_copy(
            part_ref.at[g],
            out_ref.at[:, jnp.bitwise_xor(g, xor_ref[0]), offset:offset + step],
            sems.at[g],
        )
        for g in range(irreps)
    ]
    for copy in copies:
        copy.start()
    for copy in copies:
        copy.wait()


def place_irreps(part, pair_xor, rows, offset, result):
    irreps, js, step, cols = part.shape
    operands = [pair_xor.reshape(1), part]
    aliases = {}
    if result is not None:
        aliases = {len(operands): 0}
        operands.append(result)
    return pl.pallas_call(
        functools.partial(place_body, offset),
        out_shape=jax.ShapeDtypeStruct((js, irreps, rows, cols), part.dtype),
        in_specs=[pl.BlockSpec(memory_space=pltpu.SMEM)]
        + [pl.BlockSpec(memory_space=pl.ANY)] * (len(operands) - 1),
        out_specs=pl.BlockSpec(memory_space=pl.ANY),
        scratch_shapes=[pltpu.SemaphoreType.DMA((irreps,))],
        input_output_aliases=aliases,
        compiler_params=params(16),
        cost_estimate=cost(0, 0),
        name="place_irreps",
    )(*operands)


def after(values, *earlier):
    return lax.optimization_barrier((values, earlier))[0]


def per_device(amplitudes, integrals, pair_irreps):
    quarters = lax.axis_size("ten") // IRREPS
    groups = [
        [g * quarters + (q ^ (g % 2 * quarters // 2)) for g in range(IRREPS)] for q in range(quarters)
    ]
    ranks = lax.axis_size("rep")
    quarter = lax.axis_index("ten") % quarters
    nk, rows = amplitudes.shape[1], amplitudes.shape[3]

    by_j = integrals_by_j(integrals, ranks)
    amplitudes, by_j = lax.optimization_barrier((amplitudes, by_j))
    amps = amplitudes.reshape(nk, IRREPS, rows, rows)
    by_group = order_amps(amps, pair_irreps, 0, STEPS[0])

    near = by_j[0]
    arrived = [near, shift_rep(by_j[1], 1), shift_rep(by_j[3], -1), shift_rep(by_j[2], 2)]
    by_group2 = order_amps(after(amps, arrived[1]), pair_irreps, STEPS[0], STEPS[1])
    arrived[2], by_group2 = lax.optimization_barrier((arrived[2], by_group2))
    zl = [flip_ten(part, 2) for part in arrived]
    core = [flip_ten(part, 1) for part in arrived]
    both = [flip_ten(part, 1) for part in zl]

    first = exchange_irreps(by_group, groups)
    first, near, core[1], core[2], zl[0], by_group2 = lax.optimization_barrier(
        (first, near, core[1], core[2], zl[0], by_group2)
    )
    core[0], both[0] = flip_ten(near, 1), flip_ten(zl[0], 1)
    by_group2, core[0], core[3] = lax.optimization_barrier((by_group2, core[0], core[3]))
    second = exchange_irreps(by_group2, groups)

    left, right = shift_rep(first, 1), shift_rep(first, -1)
    right2 = shift_rep(second, -1)
    left, right, zl[1] = lax.optimization_barrier((left, right, zl[1]))
    far = shift_rep(left, 1)
    both[1] = flip_ten(zl[1], 1)
    left2 = shift_rep(after(second, both[1]), 1)
    far2 = shift_rep(right2, -1)
    both[2], both[3] = flip_ten(zl[2], 1), flip_ten(zl[3], 1)
    chosen = [(arrived[n], core[n], zl[n], both[n]) for n in range(ranks)]

    (sums,) = product((first, left, right), (0, 1, 2), chosen, quarter, last=False)
    far, sums = lax.optimization_barrier((far, sums))
    (out,) = product((far,), (3,), chosen, quarter, sums=sums)
    back = exchange_irreps(out, groups)
    sums, held = product((second, right2), (0, 2), chosen, quarter, last=False, hold=(1, 3))
    left2, far2, sums, held = lax.optimization_barrier((left2, far2, sums, held))
    (out2,) = product((left2, far2), (1, 3), held, quarter, sums=sums)
    pair_xor = jnp.bitwise_xor(pair_irreps[0], pair_irreps[1])
    back, out2 = lax.optimization_barrier((back, out2))
    back2 = exchange_irreps(out2, groups)
    result = place_irreps(back, pair_xor, rows, 0, None)
    result = place_irreps(back2, pair_xor, rows, STEPS[0], result)
    return result.reshape(amplitudes.shape)


def solution(mesh):
    in_specs = (P("ten", "rep", None, None), P("rep", "ten", None, None), P())
    return jax.shard_map(
        per_device, mesh=mesh, in_specs=in_specs, out_specs=in_specs[0], check_vma=False
    )
```
